32 devices in a mesh: tm: 8 (over y, x, core), height: 4 (over z).
Axes of the slice: x: 2, y: 2, z: 4, core: 2. Of those that a mesh axis runs over, the one named last changes fastest.
Arguments:
- query_band: bfloat16 [24, 24, 24, 2048], P('tm', 'height'), may hold values from -4.5 to 4.5
- key_band: bfloat16 [24, 24, 24, 2048], P('tm', 'height'), may hold values from -11 to 11
- value_band: bfloat16 [24, 24, 24, 2048], P('tm', 'height'), may hold values from -6 to 6
Outputs:
- attended: bfloat16 [24, 24, 24, 2048], P('tm', 'height')
The draws below stay inside these ranges and needn't reach their ends.
All inputs are finite; a program needn't handle non-finite values.
Results may differ from the reference program's by a relative error of at most 0.0033.
Values may be sent and summed in bfloat16 or wider, within the bound.
A program may use at most 128 MiB of HBM per device.

```python
import jax
import jax.numpy as jnp
from jax import lax

HEADS = 16
HEAD_DIM = 128
TILE_T = 6
TILE_H = 8
TILE_W = 8
FEAT = 2048
FRAMES = 24
ROWS = 24
COLS = 24


def draw_query_band(key, part):
    key = jax.random.fold_in(key, 1)
    grid_shape = (FRAMES, ROWS, COLS, HEADS * HEAD_DIM)
    drawn = jnp.clip(jax.random.normal(key, grid_shape, jnp.float32), -4.5, 4.5)
    return drawn.astype(jnp.bfloat16)


def draw_key_band(key, part):
    key = jax.random.fold_in(key, 2)
    grid_shape = (FRAMES, ROWS, COLS, HEADS * HEAD_DIM)
    drawn = jnp.clip(2.5 * jax.random.normal(key, grid_shape, jnp.float32), -11.0, 11.0)
    return drawn.astype(jnp.bfloat16)


def level_of(key, dims, shards, low, top_value):
    level = 1.0
    for position, blocks in shards:
        steps = jax.random.uniform(jax.random.fold_in(jax.random.fold_in(key, 6), position), (blocks,), jnp.float32, low / len(shards), top_value / len(shards))
        level = level * jnp.repeat(jnp.exp(steps), dims[position] // blocks).reshape((-1,) + (1,) * (len(dims) - 1 - position))
    return level


def noise(key, extent, scale, most, cuts=(), kind=jnp.bfloat16):
    level = level_of(key, extent, cuts, -0.22, 0.18) if cuts else 1.0
    values = jax.random.normal(key, extent, jnp.float32) * scale * level
    return jnp.minimum(jnp.maximum(values, -most), most).astype(kind)


def setup_inputs(seed: int = 0) -> dict:
    seeds = jax.random.split(jax.random.key(seed), 4)
    query_band = draw_query_band(jax.random.fold_in(seeds[3], 71), 0)
    key_band = draw_key_band(jax.random.fold_in(seeds[3], 71), 0)
    value_band = noise(seeds[2], (FRAMES, ROWS, COLS, FEAT), 1.0, 6.0, ((0, 8), (1, 4)))
    return dict(query_band=query_band, key_band=key_band, value_band=value_band)


def attend_tile(queries, key_rows, value_rows, usable):
    def one_head(head_index):
        first_column = head_index * HEAD_DIM
        query_part = lax.dynamic_slice_in_dim(queries, first_column, HEAD_DIM, 1)
        key_part = lax.dynamic_slice_in_dim(key_rows, first_column, HEAD_DIM, 1)
        value_part = lax.dynamic_slice_in_dim(value_rows, first_column, HEAD_DIM, 1)
        scores = lax.dot_general(query_part, key_part, (((1,), (1,)), ((), ())), preferred_element_type=jnp.float32) * (HEAD_DIM ** -0.5)
        scores = jnp.where(usable[None, :], scores, jnp.float32(-1e30))
        largest = jnp.max(scores, axis=1, keepdims=True)
        weights = lax.optimization_barrier(jnp.exp(scores - largest).astype(jnp.bfloat16))
        weight_sum = jnp.sum(weights.astype(jnp.float32), axis=1, keepdims=True)
        return jnp.dot(weights, value_part, preferred_element_type=jnp.float32) / weight_sum

    stacked = lax.map(one_head, jnp.arange(HEADS, dtype=jnp.int32))
    return jnp.transpose(stacked, (1, 0, 2)).reshape(queries.shape[0], HEADS * HEAD_DIM).astype(jnp.bfloat16)


def reference(query_band, key_band, value_band):
    time_tiles = FRAMES // TILE_T
    row_tiles = ROWS // TILE_H
    col_tiles = COLS // TILE_W
    feature_count = HEADS * HEAD_DIM
    zero_index = jnp.zeros((), jnp.int32)
    frame_local = jnp.arange(3 * TILE_T, dtype=jnp.int32) // TILE_T
    row_local = jnp.arange(3 * TILE_H, dtype=jnp.int32) // TILE_H
    col_local = jnp.arange(3 * TILE_W, dtype=jnp.int32) // TILE_W
    grid_shape = (3 * TILE_T, 3 * TILE_H, 3 * TILE_W)

    def one_tile(tile_id):
        time_index = (tile_id // (row_tiles * col_tiles)).astype(jnp.int32)
        row_index = ((tile_id // col_tiles) % row_tiles).astype(jnp.int32)
        col_index = (tile_id % col_tiles).astype(jnp.int32)
        start_time = jnp.clip(time_index - 1, 0, time_tiles - 3).astype(jnp.int32)
        start_row = jnp.clip(row_index - 1, 0, row_tiles - 3).astype(jnp.int32)
        start_col = jnp.clip(col_index - 1, 0, col_tiles - 3).astype(jnp.int32)
        tile_queries = lax.dynamic_slice(query_band, (time_index * TILE_T, row_index * TILE_H, col_index * TILE_W, zero_index), (TILE_T, TILE_H, TILE_W, feature_count)).reshape(-1, feature_count)
        corner = (start_time * TILE_T, start_row * TILE_H, start_col * TILE_W, zero_index)
        key_rows = lax.dynamic_slice(key_band, corner, (3 * TILE_T, 3 * TILE_H, 3 * TILE_W, feature_count)).reshape(-1, feature_count)
        value_rows = lax.dynamic_slice(value_band, corner, (3 * TILE_T, 3 * TILE_H, 3 * TILE_W, feature_count)).reshape(-1, feature_count)
        time_near = jnp.abs(start_time + frame_local - time_index) <= 1
        row_near = jnp.abs(start_row + row_local - row_index) <= 1
        col_near = jnp.abs(start_col + col_local - col_index) <= 1
        usable = jnp.broadcast_to(time_near[:, None, None] & row_near[None, :, None] & col_near[None, None, :], grid_shape).reshape(-1)
        return attend_tile(tile_queries, key_rows, value_rows, usable)

    results = lax.map(one_tile, jnp.arange(time_tiles * row_tiles * col_tiles, dtype=jnp.int32))
    results = results.reshape(time_tiles, row_tiles, col_tiles, TILE_T, TILE_H, TILE_W, feature_count)
    return jnp.transpose(results, (0, 3, 1, 4, 2, 5, 6)).reshape(FRAMES, ROWS, COLS, feature_count)
```

```python
import functools
import math

import jax
import jax.numpy as jnp
from jax import lax
from jax.experimental import pallas as pl
from jax.experimental.pallas import tpu as pltpu
from jax.sharding import PartitionSpec as P

HEAD_DIM = 128
TILE_T = 6
TILE_H = 8
TILE_W = 8
MESH = pl.DeviceIdType.MESH

KEY_BLOCK = (0, 1, 5)
VALUE_BLOCK = (2, 3, 6)
QUERY_BLOCK = (4, 7, 8)
ORDER = (("k", 0), ("k", 1), ("v", 0), ("v", 1), ("q", 0), ("k", 2), ("v", 2), ("q", 1), ("q", 2))
PHASES = ((0, 5), (5, 4))
HALO = ((0, 4), (5, 2))


def kernel(dims, x_ref, out_ref, y, o, scores, send, recv, osend, orecv, hsend, hrecv):
    heads, tm, height, frames, rows, tall = dims
    heads_here = heads // height
    group = tm // heads_here
    own = heads_here
    tiles = own * frames // TILE_T
    piece = frames * rows * TILE_W
    unit = frames * TILE_H * TILE_W
    scale = HEAD_DIM ** (-0.5) * math.log2(math.e)

    me_t, me_z = lax.axis_index("tm"), lax.axis_index("height")
    part = lax.rem(me_t, group)
    my_head = me_z * heads_here + me_t // group
    my_part = me_t // own
    my_slot = lax.rem(me_t, own)
    me = me_t * height + me_z

    barrier = pltpu.get_barrier_semaphore()

    def greet(step, carry):
        other = lax.rem(me + step, tm * height)
        pl.semaphore_signal(
            barrier,
            inc=1,
            device_id={"tm": other // height, "height": lax.rem(other, height)},
            device_id_type=MESH,
        )
        return carry

    lax.fori_loop(1, tm * height, greet, 0)
    pl.semaphore_wait(barrier, tm * height - 1)

    def sending(phase, head):
        first, count = PHASES[phase]
        return pltpu.make_async_remote_copy(
            src_ref=x_ref.at[head, pl.ds(first, count)],
            dst_ref=y.at[pl.ds(first, count), 2 + my_slot, pl.ds(me_z * piece, piece), :],
            send_sem=send.at[phase, head],
            recv_sem=recv.at[phase, my_slot * height + me_z],
            device_id={"tm": lax.rem(head, heads_here) * group + my_part, "height": head // heads_here},
            device_id_type=MESH,
        )

    def keeping(phase):
        first, count = PHASES[phase]
        return pltpu.make_async_copy(
            x_ref.at[my_head, pl.ds(first, count)],
            y.at[pl.ds(first, count), 2 + my_slot, pl.ds(me_z * piece, piece), :],
            recv.at[phase, my_slot * height + me_z],
        )

    def is_me(head):
        return (head == my_head) & (part == my_part)

    def start_phase(phase):
        def one(step, carry):
            head = lax.rem(my_head + step, heads)

            @pl.when(jnp.logical_not(is_me(head)))
            def _():
                sending(phase, head).start()

            @pl.when(is_me(head))
            def _():
                keeping(phase).start()

            return carry

        lax.fori_loop(0, heads, one, 0)

    def finish_sends(phase):
        def one(head, carry):
            @pl.when(jnp.logical_not(is_me(head)))
            def _():
                sending(phase, head).wait_send()

            return carry

        lax.fori_loop(0, heads, one, 0)

    def receive_phase(phase):
        first, count = PHASES[phase]

        def one(source, carry):
            slot, z = source // height, lax.rem(source, height)
            mine = (part * own + slot == me_t) & (z == me_z)

            @pl.when(mine)
            def _():
                keeping(phase).wait()

            @pl.when(jnp.logical_not(mine))
            def _():
                pltpu.make_async_remote_copy(
                    src_ref=x_ref.at[0, pl.ds(first, count)],
                    dst_ref=y.at[pl.ds(first, count), 2 + slot, pl.ds(z * piece, piece), :],
                    send_sem=send.at[phase, 0],
                    recv_sem=recv.at[phase, source],
                    device_id={"tm": part * own + slot, "height": z},
                    device_id_type=MESH,
                ).wait_recv()

            return carry

        lax.fori_loop(0, own * height, one, 0)

    def halo(phase, right):
        first, count = HALO[phase]
        source, target, to = (own, 0, me_t + 1) if right else (2, own + 2, me_t - 1)
        return pltpu.make_async_remote_copy(
            src_ref=y.at[pl.ds(first, count), pl.ds(source, 2)],
            dst_ref=y.at[pl.ds(first, count), pl.ds(target, 2)],
            send_sem=hsend.at[phase, int(right)],
            recv_sem=hrecv.at[phase, int(right)],
            device_id={"tm": to},
            device_id_type=MESH,
        )

    def exchange_halo(phase):
        @pl.when(part < group - 1)
        def _():
            halo(phase, True).start()

        @pl.when(part > 0)
        def _():
            halo(phase, False).start()

        @pl.when(part < group - 1)
        def _():
            halo(phase, False).wait_recv()

        @pl.when(part > 0)
        def _():
            halo(phase, True).wait_recv()

    def finish_halo(phase):
        @pl.when(part < group - 1)
        def _():
            halo(phase, True).wait_send()

        @pl.when(part > 0)
        def _():
            halo(phase, False).wait_send()

    def attend(column, row, span, tile):
        columns = (max(column - 1, 0), min(column + 2, 3))
        first_pair = tile + jnp.where((part == 0) & (tile == 0), 1, 0)
        last_pair = tile + jnp.where((part == group - 1) & (tile == tiles - 1), 2, 3)
        width = 2 * span * unit
        at = pl.ds(pl.multiple_of(row * unit, unit), unit)
        near = pl.ds(pl.multiple_of(jnp.maximum(row - 1, 0) * unit, unit), span * unit)
        query = jnp.concatenate(
            [y[QUERY_BLOCK[column], 2 + 2 * tile + half, at, :] for half in (0, 1)], axis=0
        )

        def pair_of(block, pair):
            return jnp.concatenate([y[block, 2 * pair + half, near, :] for half in (0, 1)], axis=0)

        def place(c, pair):
            return (c - columns[0]) * 3 + pair - tile

        def score(c, largest):
            block = jnp.where(c == 2, KEY_BLOCK[2], c)

            def one(pair, largest):
                found = lax.dot_general(
                    query, pair_of(block, pair), (((1,), (1,)), ((), ())),
                    preferred_element_type=jnp.float32,
                )
                scores[place(c, pair), :, :width] = found
                for lane in range(0, width, 128):
                    largest = jnp.maximum(largest, found[:, lane : lane + 128])
                return largest

            return lax.fori_loop(first_pair, last_pair, one, largest)

        lowest = jnp.full((2 * unit, 128), -jnp.inf, jnp.float32)
        largest = lax.fori_loop(columns[0], columns[1], score, lowest)
        largest = jnp.max(largest, axis=1, keepdims=True)
        ones = jnp.ones((width, 128), jnp.bfloat16)

        def add(c, total):
            block = jnp.where(c == 2, VALUE_BLOCK[2], c + VALUE_BLOCK[0])

            def one(pair, total):
                weights = jnp.exp2((scores[place(c, pair), :, :width] - largest) * scale)
                value = jnp.concatenate([pair_of(block, pair), ones], axis=1)
                return total + jnp.dot(
                    weights.astype(jnp.bfloat16), value, preferred_element_type=jnp.float32
                )

            return lax.fori_loop(first_pair, last_pair, one, total)

        total = lax.fori_loop(columns[0], columns[1], add, jnp.zeros((2 * unit, 256), jnp.float32))
        result = (total[:, :128] / total[:, 128:]).astype(o.dtype)
        for half in (0, 1):
            o[column, 2 * tile + half, at, :] = result[half * unit : (half + 1) * unit]

    def attend_column(column):
        def one(step, carry):
            tile = jnp.where(lax.rem(part, 2) == 0, step, tiles - 1 - step)
            row_tiles = tall // TILE_H

            def edge(which, carry):
                attend(column, which * (row_tiles - 1), 2, tile)
                return carry

            def inner(row, carry):
                attend(column, row, 3, tile)
                return carry

            lax.fori_loop(0, 2, edge, 0)
            lax.fori_loop(1, row_tiles - 1, inner, 0)
            return carry

        lax.fori_loop(0, tiles, one, 0)

    def returning(column, source):
        slot, z = source // height, lax.rem(source, height)
        return pltpu.make_async_remote_copy(
            src_ref=o.at[column, slot, pl.ds(z * piece, piece), :],
            dst_ref=out_ref.at[my_head, column],
            send_sem=osend.at[column, source],
            recv_sem=orecv.at[column, my_head],
            device_id={"tm": part * own + slot, "height": z},
            device_id_type=MESH,
        )

    def returning_here(column):
        return pltpu.make_async_copy(
            o.at[column, my_slot, pl.ds(me_z * piece, piece), :],
            out_ref.at[my_head, column],
            orecv.at[column, my_head],
        )

    def source_is_me(source):
        return (part * own + source // height == me_t) & (lax.rem(source, height) == me_z)

    def return_column(column):
        def one(step, carry):
            source = lax.rem(my_slot * height + me_z + step, own * height)

            @pl.when(jnp.logical_not(source_is_me(source)))
            def _():
                returning(column, source).start()

            @pl.when(source_is_me(source))
            def _():
                returning_here(column).start()

            return carry

        lax.fori_loop(0, own * height, one, 0)

    def finish_column(column):
        def sent(source, carry):
            @pl.when(jnp.logical_not(source_is_me(source)))
            def _():
                returning(column, source).wait_send()

            return carry

        lax.fori_loop(0, own * height, sent, 0)

        def landed(head, carry):
            @pl.when(is_me(head))
            def _():
                returning_here(column).wait()

            @pl.when(jnp.logical_not(is_me(head)))
            def _():
                pltpu.make_async_remote_copy(
                    src_ref=o.at[column, 0, pl.ds(0, piece), :],
                    dst_ref=out_ref.at[head, column],
                    send_sem=osend.at[column, 0],
                    recv_sem=orecv.at[column, head],
                    device_id={"tm": lax.rem(head, heads_here) * group + my_part, "height": head // heads_here},
                    device_id_type=MESH,
                ).wait_recv()

            return carry

        lax.fori_loop(0, heads, landed, 0)

    for phase in (0, 1):
        start_phase(phase)
    receive_phase(0)
    exchange_halo(0)
    attend_column(0)
    return_column(0)
    receive_phase(1)
    exchange_halo(1)
    attend_column(1)
    return_column(1)
    attend_column(2)
    return_column(2)
    for phase in (0, 1):
        finish_sends(phase)
        finish_halo(phase)
    for column in (0, 1, 2):
        finish_column(column)


def body(query_band, key_band, value_band):
    frames, rows, cols, features = query_band.shape
    heads = features // HEAD_DIM
    tm, height = lax.axis_size("tm"), lax.axis_size("height")
    columns = cols // TILE_W
    piece = frames * rows * TILE_W
    tall = rows * height
    own = heads // height

    def by_head(value):
        value = value.reshape(frames, rows, columns, TILE_W, heads, HEAD_DIM)
        return jnp.transpose(value, (4, 2, 1, 0, 3, 5)).reshape(heads, columns, piece, HEAD_DIM)

    bands = {"q": by_head(query_band), "k": by_head(key_band), "v": by_head(value_band)}
    blocks = jnp.stack([bands[name][:, column] for name, column in ORDER], axis=1)

    unit = frames * TILE_H * TILE_W
    dims = (heads, tm, height, frames, rows, tall)
    result = pl.pallas_call(
        functools.partial(kernel, dims),
        out_shape=jax.ShapeDtypeStruct((heads, columns, piece, HEAD_DIM), jnp.bfloat16),
        in_specs=[pl.BlockSpec(memory_space=pl.ANY)],
        out_specs=pl.BlockSpec(memory_space=pl.ANY),
        scratch_shapes=[
            pltpu.VMEM((3 * columns, own + 4, piece * height, HEAD_DIM), jnp.bfloat16),
            pltpu.VMEM((columns, own, piece * height, HEAD_DIM), jnp.bfloat16),
            pltpu.VMEM((9, 2 * unit, 6 * unit), jnp.float32),
            pltpu.SemaphoreType.DMA((2, heads)),
            pltpu.SemaphoreType.DMA((2, own * height)),
            pltpu.SemaphoreType.DMA((columns, own * height)),
            pltpu.SemaphoreType.DMA((columns, heads)),
            pltpu.SemaphoreType.DMA((2, 2)),
            pltpu.SemaphoreType.DMA((2, 2)),
        ],
        compiler_params=pltpu.CompilerParams(
            collective_id=0, has_side_effects=True, vmem_limit_bytes=56 * 1024 * 1024
        ),
    )(blocks)
    result = result.reshape(heads, columns, rows, frames, TILE_W, HEAD_DIM)
    return jnp.transpose(result, (3, 2, 1, 4, 0, 5)).reshape(frames, rows, cols, features)


def solution(mesh):
    band = P("tm", "height", None, None)
    return jax.shard_map(
        body,
        mesh=mesh,
        in_specs=(band, band, band),
        out_specs=band,
        check_vma=False,
    )
```

```python
import functools
import math

import jax
import jax.numpy as jnp
from jax import lax
from jax.experimental import pallas as pl
from jax.experimental.pallas import tpu as pltpu
from jax.sharding import PartitionSpec as P

HEAD_DIM = 128
TILE_T = 6
TILE_H = 8
TILE_W = 8
MESH = pl.DeviceIdType.MESH

KEY_BLOCK = (0, 1, 5)
VALUE_BLOCK = (2, 3, 6)
QUERY_BLOCK = (4, 7, 8)
ORDER = (("k", 0), ("k", 1), ("v", 0), ("v", 1), ("q", 0), ("k", 2), ("v", 2), ("q", 1), ("q", 2))
PHASES = ((0, 5), (5, 3), (8, 1))
HALO = ((0, 4), (5, 2))


def kernel(dims, x_ref, out_ref, y, o, scores, send, recv, osend, orecv, hsend, hrecv):
    heads, tm, height, frames, rows, tall = dims
    heads_here = heads // height
    group = tm // heads_here
    own = heads_here
    tiles = own * frames // TILE_T
    piece = frames * rows * TILE_W
    unit = frames * TILE_H * TILE_W
    scale = HEAD_DIM ** (-0.5) * math.log2(math.e)

    me_t, me_z = lax.axis_index("tm"), lax.axis_index("height")
    part = lax.rem(me_t, group)
    my_head = me_z * heads_here + me_t // group
    my_part = me_t // own
    my_slot = lax.rem(me_t, own)
    me = me_t * height + me_z
    hops = sorted(range(height), key=lambda hop: abs(hop - height / 2))

    barrier = pltpu.get_barrier_semaphore()

    def greet(step, carry):
        other = lax.rem(me + step, tm * height)
        pl.semaphore_signal(
            barrier,
            inc=1,
            device_id={"tm": other // height, "height": lax.rem(other, height)},
            device_id_type=MESH,
        )
        return carry

    lax.fori_loop(1, tm * height, greet, 0)
    pl.semaphore_wait(barrier, tm * height - 1)

    def sending(phase, head):
        first, count = PHASES[phase]
        return pltpu.make_async_remote_copy(
            src_ref=x_ref.at[head, pl.ds(first, count)],
            dst_ref=y.at[pl.ds(first, count), 2 + my_slot, pl.ds(me_z * piece, piece), :],
            send_sem=send.at[phase, head],
            recv_sem=recv.at[phase, my_slot * height + me_z],
            device_id={"tm": lax.rem(head, heads_here) * group + my_part, "height": head // heads_here},
            device_id_type=MESH,
        )

    def keeping(phase):
        first, count = PHASES[phase]
        return pltpu.make_async_copy(
            x_ref.at[my_head, pl.ds(first, count)],
            y.at[pl.ds(first, count), 2 + my_slot, pl.ds(me_z * piece, piece), :],
            recv.at[phase, my_slot * height + me_z],
        )

    def is_me(head):
        return (head == my_head) & (part == my_part)

    def start_phase(phase):
        def one(step, carry):
            chip = lax.rem(me_t // group + step, heads_here)
            for hop in hops:
                head = lax.rem(me_z + hop, height) * heads_here + chip

                @pl.when(jnp.logical_not(is_me(head)))
                def _():
                    sending(phase, head).start()

                @pl.when(is_me(head))
                def _():
                    keeping(phase).start()

            return carry

        lax.fori_loop(0, heads_here, one, 0)

    def finish_sends(phase):
        def one(head, carry):
            @pl.when(jnp.logical_not(is_me(head)))
            def _():
                sending(phase, head).wait_send()

            return carry

        lax.fori_loop(0, heads, one, 0)

    def receive_phase(phase):
        first, count = PHASES[phase]

        def one(source, carry):
            slot, z = source // height, lax.rem(source, height)
            mine = (part * own + slot == me_t) & (z == me_z)

            @pl.when(mine)
            def _():
                keeping(phase).wait()

            @pl.when(jnp.logical_not(mine))
            def _():
                pltpu.make_async_remote_copy(
                    src_ref=x_ref.at[0, pl.ds(first, count)],
                    dst_ref=y.at[pl.ds(first, count), 2 + slot, pl.ds(z * piece, piece), :],
                    send_sem=send.at[phase, 0],
                    recv_sem=recv.at[phase, source],
                    device_id={"tm": part * own + slot, "height": z},
                    device_id_type=MESH,
                ).wait_recv()

            return carry

        lax.fori_loop(0, own * height, one, 0)

    def halo(phase, right):
        first, count = HALO[phase]
        source, target, to = (own, 0, me_t + 1) if right else (2, own + 2, me_t - 1)
        return pltpu.make_async_remote_copy(
            src_ref=y.at[pl.ds(first, count), pl.ds(source, 2)],
            dst_ref=y.at[pl.ds(first, count), pl.ds(target, 2)],
            send_sem=hsend.at[phase, int(right)],
            recv_sem=hrecv.at[phase, int(right)],
            device_id={"tm": to},
            device_id_type=MESH,
        )

    def exchange_halo(phase):
        @pl.when(part < group - 1)
        def _():
            halo(phase, True).start()

        @pl.when(part > 0)
        def _():
            halo(phase, False).start()

        @pl.when(part < group - 1)
        def _():
            halo(phase, False).wait_recv()

        @pl.when(part > 0)
        def _():
            halo(phase, True).wait_recv()

    def finish_halo(phase):
        @pl.when(part < group - 1)
        def _():
            halo(phase, True).wait_send()

        @pl.when(part > 0)
        def _():
            halo(phase, False).wait_send()

    def attend(column, row, span, tile):
        columns = (max(column - 1, 0), min(column + 2, 3))
        first_pair = tile + jnp.where((part == 0) & (tile == 0), 1, 0)
        last_pair = tile + jnp.where((part == group - 1) & (tile == tiles - 1), 2, 3)
        width = 2 * span * unit
        at = pl.ds(pl.multiple_of(row * unit, unit), unit)
        near = pl.ds(pl.multiple_of(jnp.maximum(row - 1, 0) * unit, unit), span * unit)
        query = jnp.concatenate(
            [y[QUERY_BLOCK[column], 2 + 2 * tile + half, at, :] for half in (0, 1)], axis=0
        )

        def pair_of(block, pair):
            return jnp.concatenate([y[block, 2 * pair + half, near, :] for half in (0, 1)], axis=0)

        def place(c, pair):
            return (c - columns[0]) * 3 + pair - tile

        def score(c, largest):
            block = jnp.where(c == 2, KEY_BLOCK[2], c)

            def one(pair, largest):
                found = lax.dot_general(
                    query, pair_of(block, pair), (((1,), (1,)), ((), ())),
                    preferred_element_type=jnp.float32,
                )
                scores[place(c, pair), :, :width] = found
                for lane in range(0, width, 128):
                    largest = jnp.maximum(largest, found[:, lane : lane + 128])
                return largest

            return lax.fori_loop(first_pair, last_pair, one, largest)

        lowest = jnp.full((2 * unit, 128), -jnp.inf, jnp.float32)
        largest = lax.fori_loop(columns[0], columns[1], score, lowest)
        largest = jnp.max(largest, axis=1, keepdims=True)
        ones = jnp.ones((width, 128), jnp.bfloat16)

        def add(c, total):
            block = jnp.where(c == 2, VALUE_BLOCK[2], c + VALUE_BLOCK[0])

            def one(pair, total):
                weights = jnp.exp2((scores[place(c, pair), :, :width] - largest) * scale)
                value = jnp.concatenate([pair_of(block, pair), ones], axis=1)
                return total + jnp.dot(
                    weights.astype(jnp.bfloat16), value, preferred_element_type=jnp.float32
                )

            return lax.fori_loop(first_pair, last_pair, one, total)

        total = lax.fori_loop(columns[0], columns[1], add, jnp.zeros((2 * unit, 256), jnp.float32))
        result = (total[:, :128] / total[:, 128:]).astype(o.dtype)
        for half in (0, 1):
            o[column, 2 * tile + half, at, :] = result[half * unit : (half + 1) * unit]

    def attend_column(column):
        def one(step, carry):
            tile = jnp.where(lax.rem(part, 2) == 0, step, tiles - 1 - step)
            row_tiles = tall // TILE_H

            def edge(which, carry):
                attend(column, which * (row_tiles - 1), 2, tile)
                return carry

            def inner(row, carry):
                attend(column, row, 3, tile)
                return carry

            lax.fori_loop(0, 2, edge, 0)
            lax.fori_loop(1, row_tiles - 1, inner, 0)
            return_tile(column, tile)
            return carry

        lax.fori_loop(0, tiles, one, 0)

    def returning(column, source):
        slot, z = source // height, lax.rem(source, height)
        return pltpu.make_async_remote_copy(
            src_ref=o.at[column, slot, pl.ds(z * piece, piece), :],
            dst_ref=out_ref.at[my_head, column],
            send_sem=osend.at[column, source],
            recv_sem=orecv.at[column, my_head],
            device_id={"tm": part * own + slot, "height": z},
            device_id_type=MESH,
        )

    def returning_here(column):
        return pltpu.make_async_copy(
            o.at[column, my_slot, pl.ds(me_z * piece, piece), :],
            out_ref.at[my_head, column],
            orecv.at[column, my_head],
        )

    def source_is_me(source):
        return (part * own + source // height == me_t) & (lax.rem(source, height) == me_z)

    def return_tile(column, tile):
        def one(step, carry):
            z = lax.rem(me_z + height // 2 + step // 2, height)
            source = (2 * tile + lax.rem(step, 2)) * height + z

            @pl.when(jnp.logical_not(source_is_me(source)))
            def _():
                returning(column, source).start()

            @pl.when(source_is_me(source))
            def _():
                returning_here(column).start()

            return carry

        lax.fori_loop(0, 2 * height, one, 0)

    def finish_column(column):
        def sent(source, carry):
            @pl.when(jnp.logical_not(source_is_me(source)))
            def _():
                returning(column, source).wait_send()

            return carry

        lax.fori_loop(0, own * height, sent, 0)

        def landed(head, carry):
            @pl.when(is_me(head))
            def _():
                returning_here(column).wait()

            @pl.when(jnp.logical_not(is_me(head)))
            def _():
                pltpu.make_async_remote_copy(
                    src_ref=o.at[column, 0, pl.ds(0, piece), :],
                    dst_ref=out_ref.at[head, column],
                    send_sem=osend.at[column, 0],
                    recv_sem=orecv.at[column, head],
                    device_id={"tm": lax.rem(head, heads_here) * group + my_part, "height": head // heads_here},
                    device_id_type=MESH,
                ).wait_recv()

            return carry

        lax.fori_loop(0, heads, landed, 0)

    for phase in range(len(PHASES)):
        start_phase(phase)
    for phase in range(len(PHASES)):
        receive_phase(phase)
        if phase < len(HALO):
            exchange_halo(phase)
        attend_column(phase)
    for phase in range(len(PHASES)):
        finish_sends(phase)
    for phase in range(len(HALO)):
        finish_halo(phase)
    for column in (0, 1, 2):
        finish_column(column)


def body(query_band, key_band, value_band):
    frames, rows, cols, features = query_band.shape
    heads = features // HEAD_DIM
    tm, height = lax.axis_size("tm"), lax.axis_size("height")
    columns = cols // TILE_W
    piece = frames * rows * TILE_W
    tall = rows * height
    own = heads // height

    def by_head(value):
        value = value.reshape(frames, rows, columns, TILE_W, heads, HEAD_DIM)
        return jnp.transpose(value, (4, 2, 1, 0, 3, 5)).reshape(heads, columns, piece, HEAD_DIM)

    bands = {"q": by_head(query_band), "k": by_head(key_band), "v": by_head(value_band)}
    blocks = jnp.stack([bands[name][:, column] for name, column in ORDER], axis=1)

    unit = frames * TILE_H * TILE_W
    dims = (heads, tm, height, frames, rows, tall)
    result = pl.pallas_call(
        functools.partial(kernel, dims),
        out_shape=jax.ShapeDtypeStruct((heads, columns, piece, HEAD_DIM), jnp.bfloat16),
        in_specs=[pl.BlockSpec(memory_space=pl.ANY)],
        out_specs=pl.BlockSpec(memory_space=pl.ANY),
        scratch_shapes=[
            pltpu.VMEM((3 * columns, own + 4, piece * height, HEAD_DIM), jnp.bfloat16),
            pltpu.VMEM((columns, own, piece * height, HEAD_DIM), jnp.bfloat16),
            pltpu.VMEM((9, 2 * unit, 6 * unit), jnp.float32),
            pltpu.SemaphoreType.DMA((len(PHASES), heads)),
            pltpu.SemaphoreType.DMA((len(PHASES), own * height)),
            pltpu.SemaphoreType.DMA((columns, own * height)),
            pltpu.SemaphoreType.DMA((columns, heads)),
            pltpu.SemaphoreType.DMA((2, 2)),
            pltpu.SemaphoreType.DMA((2, 2)),
        ],
        compiler_params=pltpu.CompilerParams(
            collective_id=0, has_side_effects=True, vmem_limit_bytes=56 * 1024 * 1024
        ),
    )(blocks)
    result = result.reshape(heads, columns, rows, frames, TILE_W, HEAD_DIM)
    return jnp.transpose(result, (3, 2, 1, 4, 0, 5)).reshape(frames, rows, cols, features)


def solution(mesh):
    band = P("tm", "height", None, None)
    return jax.shard_map(
        body,
        mesh=mesh,
        in_specs=(band, band, band),
        out_specs=band,
        check_vma=False,
    )
```

```python
import functools
import math

import jax
import jax.numpy as jnp
from jax import lax
from jax.experimental import pallas as pl
from jax.experimental.pallas import tpu as pltpu
from jax.sharding import PartitionSpec as P

HEAD_DIM = 128
TILE_T = 6
TILE_H = 8
TILE_W = 8
BLOCK = 768
MESH = pl.DeviceIdType.MESH

KEY_BLOCK = (0, 1, 5)
VALUE_BLOCK = (2, 3, 6)
QUERY_BLOCK = (4, 7, 8)
ORDER = (("k", 0), ("k", 1), ("v", 0), ("v", 1), ("q", 0), ("k", 2), ("v", 2), ("q", 1), ("q", 2))
PHASES = ((0, 5), (5, 3), (8, 1))
HALO = ((0, 4), (5, 2))


def kernel(dims, x_ref, out_ref, y, o, scores, send, recv, osend, orecv, hsend, hrecv):
    heads, tm, height, frames, rows, tall = dims
    heads_here = heads // height
    group = tm // heads_here
    own = heads_here
    tiles = own * frames // TILE_T
    piece = frames * rows * TILE_W
    unit = frames * TILE_H * TILE_W
    scale = HEAD_DIM ** (-0.5) * math.log2(math.e)

    me_t, me_z = lax.axis_index("tm"), lax.axis_index("height")
    part = lax.rem(me_t, group)
    my_head = me_z * heads_here + me_t // group
    my_part = me_t // own
    my_slot = lax.rem(me_t, own)
    me = me_t * height + me_z
    hops = sorted(range(height), key=lambda hop: abs(hop - height / 2))

    barrier = pltpu.get_barrier_semaphore()

    def greet(step, carry):
        other = lax.rem(me + step, tm * height)
        pl.semaphore_signal(
            barrier,
            inc=1,
            device_id={"tm": other // height, "height": lax.rem(other, height)},
            device_id_type=MESH,
        )
        return carry

    lax.fori_loop(1, tm * height, greet, 0)
    pl.semaphore_wait(barrier, tm * height - 1)

    def sending(phase, head):
        first, count = PHASES[phase]
        return pltpu.make_async_remote_copy(
            src_ref=x_ref.at[head, pl.ds(first, count)],
            dst_ref=y.at[pl.ds(first, count), 2 + my_slot, pl.ds(me_z * piece, piece), :],
            send_sem=send.at[phase, head],
            recv_sem=recv.at[phase, my_slot * height + me_z],
            device_id={"tm": lax.rem(head, heads_here) * group + my_part, "height": head // heads_here},
            device_id_type=MESH,
        )

    def keeping(phase):
        first, count = PHASES[phase]
        return pltpu.make_async_copy(
            x_ref.at[my_head, pl.ds(first, count)],
            y.at[pl.ds(first, count), 2 + my_slot, pl.ds(me_z * piece, piece), :],
            recv.at[phase, my_slot * height + me_z],
        )

    def is_me(head):
        return (head == my_head) & (part == my_part)

    def start_phase(phase):
        def one(step, carry):
            chip = lax.rem(me_t // group + step, heads_here)
            for hop in hops:
                head = lax.rem(me_z + hop, height) * heads_here + chip

                @pl.when(jnp.logical_not(is_me(head)))
                def _():
                    sending(phase, head).start()

                @pl.when(is_me(head))
                def _():
                    keeping(phase).start()

            return carry

        lax.fori_loop(0, heads_here, one, 0)

    def finish_sends(phase):
        def one(head, carry):
            @pl.when(jnp.logical_not(is_me(head)))
            def _():
                sending(phase, head).wait_send()

            return carry

        lax.fori_loop(0, heads, one, 0)

    def receive_phase(phase):
        first, count = PHASES[phase]

        def one(source, carry):
            slot, z = source // height, lax.rem(source, height)
            mine = (part * own + slot == me_t) & (z == me_z)

            @pl.when(mine)
            def _():
                keeping(phase).wait()

            @pl.when(jnp.logical_not(mine))
            def _():
                pltpu.make_async_remote_copy(
                    src_ref=x_ref.at[0, pl.ds(first, count)],
                    dst_ref=y.at[pl.ds(first, count), 2 + slot, pl.ds(z * piece, piece), :],
                    send_sem=send.at[phase, 0],
                    recv_sem=recv.at[phase, source],
                    device_id={"tm": part * own + slot, "height": z},
                    device_id_type=MESH,
                ).wait_recv()

            return carry

        lax.fori_loop(0, own * height, one, 0)

    def halo(phase, right):
        first, count = HALO[phase]
        source, target, to = (own, 0, me_t + 1) if right else (2, own + 2, me_t - 1)
        return pltpu.make_async_remote_copy(
            src_ref=y.at[pl.ds(first, count), pl.ds(source, 2)],
            dst_ref=y.at[pl.ds(first, count), pl.ds(target, 2)],
            send_sem=hsend.at[phase, int(right)],
            recv_sem=hrecv.at[phase, int(right)],
            device_id={"tm": to},
            device_id_type=MESH,
        )

    def exchange_halo(phase):
        @pl.when(part < group - 1)
        def _():
            halo(phase, True).start()

        @pl.when(part > 0)
        def _():
            halo(phase, False).start()

        @pl.when(part < group - 1)
        def _():
            halo(phase, False).wait_recv()

        @pl.when(part > 0)
        def _():
            halo(phase, True).wait_recv()

    def finish_halo(phase):
        @pl.when(part < group - 1)
        def _():
            halo(phase, True).wait_send()

        @pl.when(part > 0)
        def _():
            halo(phase, False).wait_send()

    def attend(column, row, span, tile):
        columns = (max(column - 1, 0), min(column + 2, 3))
        first_pair = tile + jnp.where((part == 0) & (tile == 0), 1, 0)
        last_pair = tile + jnp.where((part == group - 1) & (tile == tiles - 1), 2, 3)
        width = 2 * span * unit
        at = pl.ds(pl.multiple_of(row * unit, unit), unit)
        near = pl.ds(pl.multiple_of(jnp.maximum(row - 1, 0) * unit, unit), span * unit)
        query = jnp.concatenate(
            [y[QUERY_BLOCK[column], 2 + 2 * tile + half, at, :] for half in (0, 1)], axis=0
        )

        def pair_of(block, pair):
            return jnp.concatenate([y[block, 2 * pair + half, near, :] for half in (0, 1)], axis=0)

        across = range(columns[0], columns[1])
        blocks = [(low, min(low + BLOCK, width * len(across))) for low in range(0, width * len(across), BLOCK)]

        def score(pair, largest):
            keys = jnp.concatenate([pair_of(KEY_BLOCK[c], pair) for c in across], axis=0)
            for low, high in blocks:
                found = lax.dot_general(
                    query, keys[low:high], (((1,), (1,)), ((), ())), preferred_element_type=jnp.float32
                )
                scores[pair - tile, :, low:high] = found
                for lane in range(0, high - low, 128):
                    largest = jnp.maximum(largest, found[:, lane : lane + 128])
            return largest

        lowest = jnp.full((2 * unit, 128), -jnp.inf, jnp.float32)
        largest = lax.fori_loop(first_pair, last_pair, score, lowest)
        largest = jnp.max(largest, axis=1, keepdims=True)

        def weigh(pair, block):
            low, high = block
            return jnp.exp2((scores[pair - tile, :, low:high] - largest) * scale).astype(jnp.bfloat16)

        def add(pair, total):
            values = jnp.concatenate([pair_of(VALUE_BLOCK[c], pair) for c in across], axis=0)
            weights = weigh(pair, blocks[0])
            for index, (low, high) in enumerate(blocks):
                current = weights
                if index + 1 < len(blocks):
                    weights = weigh(pair, blocks[index + 1])
                value = jnp.concatenate([values[low:high], jnp.ones((high - low, 128), jnp.bfloat16)], axis=1)
                total = total + jnp.dot(current, value, preferred_element_type=jnp.float32)
            return total

        total = lax.fori_loop(first_pair, last_pair, add, jnp.zeros((2 * unit, 256), jnp.float32))
        result = (total[:, :128] / total[:, 128:]).astype(o.dtype)
        for half in (0, 1):
            o[column, 2 * tile + half, at, :] = result[half * unit : (half + 1) * unit]

    def attend_column(column):
        def one(step, carry):
            tile = jnp.where(lax.rem(part, 2) == 0, step, tiles - 1 - step)
            row_tiles = tall // TILE_H

            def edge(which, carry):
                attend(column, which * (row_tiles - 1), 2, tile)
                return carry

            def inner(row, carry):
                attend(column, row, 3, tile)
                return carry

            lax.fori_loop(0, 2, edge, 0)
            lax.fori_loop(1, row_tiles - 1, inner, 0)
            return_tile(column, tile)
            return carry

        lax.fori_loop(0, tiles, one, 0)

    def returning(column, source):
        slot, z = source // height, lax.rem(source, height)
        return pltpu.make_async_remote_copy(
            src_ref=o.at[column, slot, pl.ds(z * piece, piece), :],
            dst_ref=out_ref.at[my_head, column],
            send_sem=osend.at[column, source],
            recv_sem=orecv.at[column, my_head],
            device_id={"tm": part * own + slot, "height": z},
            device_id_type=MESH,
        )

    def returning_here(column):
        return pltpu.make_async_copy(
            o.at[column, my_slot, pl.ds(me_z * piece, piece), :],
            out_ref.at[my_head, column],
            orecv.at[column, my_head],
        )

    def source_is_me(source):
        return (part * own + source // height == me_t) & (lax.rem(source, height) == me_z)

    def return_tile(column, tile):
        def one(step, carry):
            z = lax.rem(me_z + height // 2 + step // 2, height)
            source = (2 * tile + lax.rem(step, 2)) * height + z

            @pl.when(jnp.logical_not(source_is_me(source)))
            def _():
                returning(column, source).start()

            @pl.when(source_is_me(source))
            def _():
                returning_here(column).start()

            return carry

        lax.fori_loop(0, 2 * height, one, 0)

    def finish_column(column):
        def sent(source, carry):
            @pl.when(jnp.logical_not(source_is_me(source)))
            def _():
                returning(column, source).wait_send()

            return carry

        lax.fori_loop(0, own * height, sent, 0)

        def landed(head, carry):
            @pl.when(is_me(head))
            def _():
                returning_here(column).wait()

            @pl.when(jnp.logical_not(is_me(head)))
            def _():
                pltpu.make_async_remote_copy(
                    src_ref=o.at[column, 0, pl.ds(0, piece), :],
                    dst_ref=out_ref.at[head, column],
                    send_sem=osend.at[column, 0],
                    recv_sem=orecv.at[column, head],
                    device_id={"tm": lax.rem(head, heads_here) * group + my_part, "height": head // heads_here},
                    device_id_type=MESH,
                ).wait_recv()

            return carry

        lax.fori_loop(0, heads, landed, 0)

    for phase in range(len(PHASES)):
        start_phase(phase)
    for phase in range(len(PHASES)):
        receive_phase(phase)
        if phase < len(HALO):
            exchange_halo(phase)
        attend_column(phase)
    for phase in range(len(PHASES)):
        finish_sends(phase)
    for phase in range(len(HALO)):
        finish_halo(phase)
    for column in (0, 1, 2):
        finish_column(column)


def body(query_band, key_band, value_band):
    frames, rows, cols, features = query_band.shape
    heads = features // HEAD_DIM
    tm, height = lax.axis_size("tm"), lax.axis_size("height")
    columns = cols // TILE_W
    piece = frames * rows * TILE_W
    tall = rows * height
    own = heads // height

    def by_head(value):
        value = value.reshape(frames, rows, columns, TILE_W, heads, HEAD_DIM)
        return jnp.transpose(value, (4, 2, 1, 0, 3, 5)).reshape(heads, columns, piece, HEAD_DIM)

    bands = {"q": by_head(query_band), "k": by_head(key_band), "v": by_head(value_band)}
    blocks = jnp.stack([bands[name][:, column] for name, column in ORDER], axis=1)

    unit = frames * TILE_H * TILE_W
    dims = (heads, tm, height, frames, rows, tall)
    result = pl.pallas_call(
        functools.partial(kernel, dims),
        out_shape=jax.ShapeDtypeStruct((heads, columns, piece, HEAD_DIM), jnp.bfloat16),
        in_specs=[pl.BlockSpec(memory_space=pl.ANY)],
        out_specs=pl.BlockSpec(memory_space=pl.ANY),
        scratch_shapes=[
            pltpu.VMEM((3 * columns, own + 4, piece * height, HEAD_DIM), jnp.bfloat16),
            pltpu.VMEM((columns, own, piece * height, HEAD_DIM), jnp.bfloat16),
            pltpu.VMEM((3, 2 * unit, 18 * unit), jnp.float32),
            pltpu.SemaphoreType.DMA((len(PHASES), heads)),
            pltpu.SemaphoreType.DMA((len(PHASES), own * height)),
            pltpu.SemaphoreType.DMA((columns, own * height)),
            pltpu.SemaphoreType.DMA((columns, heads)),
            pltpu.SemaphoreType.DMA((2, 2)),
            pltpu.SemaphoreType.DMA((2, 2)),
        ],
        compiler_params=pltpu.CompilerParams(
            collective_id=0, has_side_effects=True, vmem_limit_bytes=56 * 1024 * 1024
        ),
    )(blocks)
    result = result.reshape(heads, columns, rows, frames, TILE_W, HEAD_DIM)
    return jnp.transpose(result, (3, 2, 1, 4, 0, 5)).reshape(frames, rows, cols, features)


def solution(mesh):
    band = P("tm", "height", None, None)
    return jax.shard_map(
        body,
        mesh=mesh,
        in_specs=(band, band, band),
        out_specs=band,
        check_vma=False,
    )
```

```python
import functools
import math

import jax
import jax.numpy as jnp
from jax import lax
from jax.experimental import pallas as pl
from jax.experimental.pallas import tpu as pltpu
from jax.sharding import PartitionSpec as P

HEAD_DIM = 128
TILE_T = 6
TILE_H = 8
TILE_W = 8
BLOCK = 768
MESH = pl.DeviceIdType.MESH

KEY_BLOCK = (0, 1, 5)
VALUE_BLOCK = (2, 3, 6)
QUERY_BLOCK = (4, 7, 8)
ORDER = (("k", 0), ("k", 1), ("v", 0), ("v", 1), ("q", 0), ("k", 2), ("v", 2), ("q", 1), ("q", 2))
PHASES = ((0, 5), (5, 3), (8, 1))
HALO = ((0, 4), (5, 2))


def kernel(dims, x_ref, out_ref, y, o, scores, peak, edge_keys, inner_keys, send, recv, osend, orecv, hsend, hrecv):
    heads, tm, height, frames, rows, tall = dims
    heads_here = heads // height
    group = tm // heads_here
    own = heads_here
    tiles = own * frames // TILE_T
    piece = frames * rows * TILE_W
    unit = frames * TILE_H * TILE_W
    scale = HEAD_DIM ** (-0.5) * math.log2(math.e)

    me_t, me_z = lax.axis_index("tm"), lax.axis_index("height")
    part = lax.rem(me_t, group)
    my_head = me_z * heads_here + me_t // group
    my_part = me_t // own
    my_slot = lax.rem(me_t, own)
    me = me_t * height + me_z
    hops = sorted(range(height), key=lambda hop: abs(hop - height / 2))

    barrier = pltpu.get_barrier_semaphore()

    def greet(step, carry):
        other = lax.rem(me + step, tm * height)
        pl.semaphore_signal(
            barrier,
            inc=1,
            device_id={"tm": other // height, "height": lax.rem(other, height)},
            device_id_type=MESH,
        )
        return carry

    lax.fori_loop(1, tm * height, greet, 0)
    pl.semaphore_wait(barrier, tm * height - 1)

    def sending(phase, head):
        first, count = PHASES[phase]
        return pltpu.make_async_remote_copy(
            src_ref=x_ref.at[head, pl.ds(first, count)],
            dst_ref=y.at[pl.ds(first, count), 2 + my_slot, pl.ds(me_z * piece, piece), :],
            send_sem=send.at[phase, head],
            recv_sem=recv.at[phase, my_slot * height + me_z],
            device_id={"tm": lax.rem(head, heads_here) * group + my_part, "height": head // heads_here},
            device_id_type=MESH,
        )

    def keeping(phase):
        first, count = PHASES[phase]
        return pltpu.make_async_copy(
            x_ref.at[my_head, pl.ds(first, count)],
            y.at[pl.ds(first, count), 2 + my_slot, pl.ds(me_z * piece, piece), :],
            recv.at[phase, my_slot * height + me_z],
        )

    def is_me(head):
        return (head == my_head) & (part == my_part)

    def start_phase(phase):
        def one(step, carry):
            chip = lax.rem(me_t // group + step, heads_here)
            for hop in hops:
                head = lax.rem(me_z + hop, height) * heads_here + chip

                @pl.when(jnp.logical_not(is_me(head)))
                def _():
                    sending(phase, head).start()

                @pl.when(is_me(head))
                def _():
                    keeping(phase).start()

            return carry

        lax.fori_loop(0, heads_here, one, 0)

    def finish_sends(phase):
        def one(head, carry):
            @pl.when(jnp.logical_not(is_me(head)))
            def _():
                sending(phase, head).wait_send()

            return carry

        lax.fori_loop(0, heads, one, 0)

    def receive_phase(phase):
        first, count = PHASES[phase]

        def one(source, carry):
            slot, z = source // height, lax.rem(source, height)
            mine = (part * own + slot == me_t) & (z == me_z)

            @pl.when(mine)
            def _():
                keeping(phase).wait()

            @pl.when(jnp.logical_not(mine))
            def _():
                pltpu.make_async_remote_copy(
                    src_ref=x_ref.at[0, pl.ds(first, count)],
                    dst_ref=y.at[pl.ds(first, count), 2 + slot, pl.ds(z * piece, piece), :],
                    send_sem=send.at[phase, 0],
                    recv_sem=recv.at[phase, source],
                    device_id={"tm": part * own + slot, "height": z},
                    device_id_type=MESH,
                ).wait_recv()

            return carry

        lax.fori_loop(0, own * height, one, 0)

    def halo(phase, right):
        first, count = HALO[phase]
        source, target, to = (own, 0, me_t + 1) if right else (2, own + 2, me_t - 1)
        return pltpu.make_async_remote_copy(
            src_ref=y.at[pl.ds(first, count), pl.ds(source, 2)],
            dst_ref=y.at[pl.ds(first, count), pl.ds(target, 2)],
            send_sem=hsend.at[phase, int(right)],
            recv_sem=hrecv.at[phase, int(right)],
            device_id={"tm": to},
            device_id_type=MESH,
        )

    def exchange_halo(phase):
        @pl.when(part < group - 1)
        def _():
            halo(phase, True).start()

        @pl.when(part > 0)
        def _():
            halo(phase, False).start()

        @pl.when(part < group - 1)
        def _():
            halo(phase, False).wait_recv()

        @pl.when(part > 0)
        def _():
            halo(phase, True).wait_recv()

    def finish_halo(phase):
        @pl.when(part < group - 1)
        def _():
            halo(phase, True).wait_send()

        @pl.when(part > 0)
        def _():
            halo(phase, False).wait_send()

    def turn_keys(new):
        def one(pair, carry):
            for c in new:
                first, second = (y[KEY_BLOCK[c], 2 * pair + half] for half in (0, 1))
                for which, low in enumerate((0, unit)):
                    both = jnp.concatenate([first[low : low + 2 * unit], second[low : low + 2 * unit]], axis=0)
                    edge_keys[which, c, pair] = both.T
                inner_keys[c, pair] = jnp.concatenate([first, second], axis=0).T
            return carry

        first_pair = jnp.where(part == 0, 1, 0)
        last_pair = tiles + jnp.where(part == group - 1, 1, 2)
        lax.fori_loop(first_pair, last_pair, one, 0)

    def attend(column, row, span, tile):
        columns = (max(column - 1, 0), min(column + 2, 3))
        first_pair = tile + jnp.where((part == 0) & (tile == 0), 1, 0)
        last_pair = tile + jnp.where((part == group - 1) & (tile == tiles - 1), 2, 3)
        width = 2 * span * unit
        at = pl.ds(pl.multiple_of(row * unit, unit), unit)
        near = pl.ds(pl.multiple_of(jnp.maximum(row - 1, 0) * unit, unit), span * unit)
        query = jnp.concatenate(
            [y[QUERY_BLOCK[column], 2 + 2 * tile + half, at, :] for half in (0, 1)], axis=0
        )

        def pair_of(block, pair):
            return jnp.concatenate([y[block, 2 * pair + half, near, :] for half in (0, 1)], axis=0)

        across = range(columns[0], columns[1])
        blocks = [(low, min(low + BLOCK, width * len(across))) for low in range(0, width * len(across), BLOCK)]

        def turned(c, pair):
            return edge_keys[lax.div(row, 2), c, pair] if span == 2 else inner_keys[c, pair]

        def score(pair, largest):
            keys = jnp.concatenate([turned(c, pair) for c in across], axis=1)
            for low, high in blocks:
                found = jnp.dot(query, keys[:, low:high], preferred_element_type=jnp.float32)
                scores[pair - tile, :, low:high] = found
                for lane in range(0, high - low, 128):
                    largest = jnp.maximum(largest, found[:, lane : lane + 128])
            return largest

        lowest = jnp.full((2 * unit, 128), -jnp.inf, jnp.float32)
        largest = lax.fori_loop(first_pair, last_pair, score, lowest)
        peak[...] = jnp.broadcast_to(jnp.max(largest, axis=1, keepdims=True), peak.shape)

        def weigh(pair, block):
            top = peak[...]
            parts = [
                jnp.exp2((scores[pair - tile, :, lane : lane + 128] - top) * scale).astype(jnp.bfloat16)
                for lane in range(block[0], block[1], 128)
            ]
            return jnp.concatenate(parts, axis=1)

        def add(pair, total):
            values = jnp.concatenate([pair_of(VALUE_BLOCK[c], pair) for c in across], axis=0)
            weights = weigh(pair, blocks[0])
            for index, (low, high) in enumerate(blocks):
                current = weights
                if index + 1 < len(blocks):
                    weights = weigh(pair, blocks[index + 1])
                value = jnp.concatenate([values[low:high], jnp.ones((high - low, 128), jnp.bfloat16)], axis=1)
                total = total + jnp.dot(current, value, preferred_element_type=jnp.float32)
            return total

        total = lax.fori_loop(first_pair, last_pair, add, jnp.zeros((2 * unit, 256), jnp.float32))
        result = (total[:, :128] / total[:, 128:]).astype(o.dtype)
        for half in (0, 1):
            o[column, 2 * tile + half, at, :] = result[half * unit : (half + 1) * unit]

    def attend_column(column):
        def one(step, carry):
            tile = jnp.where(lax.rem(part, 2) == 0, step, tiles - 1 - step)
            row_tiles = tall // TILE_H

            def edge(which, carry):
                attend(column, which * (row_tiles - 1), 2, tile)
                return carry

            def inner(row, carry):
                attend(column, row, 3, tile)
                return carry

            lax.fori_loop(0, 2, edge, 0)
            lax.fori_loop(1, row_tiles - 1, inner, 0)
            return_tile(column, tile)
            return carry

        lax.fori_loop(0, tiles, one, 0)

    def returning(column, source):
        slot, z = source // height, lax.rem(source, height)
        return pltpu.make_async_remote_copy(
            src_ref=o.at[column, slot, pl.ds(z * piece, piece), :],
            dst_ref=out_ref.at[my_head, column],
            send_sem=osend.at[column, source],
            recv_sem=orecv.at[column, my_head],
            device_id={"tm": part * own + slot, "height": z},
            device_id_type=MESH,
        )

    def returning_here(column):
        return pltpu.make_async_copy(
            o.at[column, my_slot, pl.ds(me_z * piece, piece), :],
            out_ref.at[my_head, column],
            orecv.at[column, my_head],
        )

    def source_is_me(source):
        return (part * own + source // height == me_t) & (lax.rem(source, height) == me_z)

    def return_tile(column, tile):
        def one(step, carry):
            z = lax.rem(me_z + height // 2 + step // 2, height)
            source = (2 * tile + lax.rem(step, 2)) * height + z

            @pl.when(jnp.logical_not(source_is_me(source)))
            def _():
                returning(column, source).start()

            @pl.when(source_is_me(source))
            def _():
                returning_here(column).start()

            return carry

        lax.fori_loop(0, 2 * height, one, 0)

    def finish_column(column):
        def sent(source, carry):
            @pl.when(jnp.logical_not(source_is_me(source)))
            def _():
                returning(column, source).wait_send()

            return carry

        lax.fori_loop(0, own * height, sent, 0)

        def landed(head, carry):
            @pl.when(is_me(head))
            def _():
                returning_here(column).wait()

            @pl.when(jnp.logical_not(is_me(head)))
            def _():
                pltpu.make_async_remote_copy(
                    src_ref=o.at[column, 0, pl.ds(0, piece), :],
                    dst_ref=out_ref.at[head, column],
                    send_sem=osend.at[column, 0],
                    recv_sem=orecv.at[column, head],
                    device_id={"tm": lax.rem(head, heads_here) * group + my_part, "height": head // heads_here},
                    device_id_type=MESH,
                ).wait_recv()

            return carry

        lax.fori_loop(0, heads, landed, 0)

    for phase in range(len(PHASES)):
        start_phase(phase)
    for phase in range(len(PHASES)):
        receive_phase(phase)
        if phase < len(HALO):
            exchange_halo(phase)
            turn_keys(((0, 1), (2,))[phase])
        attend_column(phase)
    for phase in range(len(PHASES)):
        finish_sends(phase)
    for phase in range(len(HALO)):
        finish_halo(phase)
    for column in (0, 1, 2):
        finish_column(column)


def body(query_band, key_band, value_band):
    frames, rows, cols, features = query_band.shape
    heads = features // HEAD_DIM
    tm, height = lax.axis_size("tm"), lax.axis_size("height")
    columns = cols // TILE_W
    piece = frames * rows * TILE_W
    tall = rows * height
    own = heads // height

    def by_head(value):
        value = value.reshape(frames, rows, columns, TILE_W, heads, HEAD_DIM)
        return jnp.transpose(value, (4, 2, 1, 0, 3, 5)).reshape(heads, columns, piece, HEAD_DIM)

    bands = {"q": by_head(query_band), "k": by_head(key_band), "v": by_head(value_band)}
    blocks = jnp.stack([bands[name][:, column] for name, column in ORDER], axis=1)

    unit = frames * TILE_H * TILE_W
    dims = (heads, tm, height, frames, rows, tall)
    result = pl.pallas_call(
        functools.partial(kernel, dims),
        out_shape=jax.ShapeDtypeStruct((heads, columns, piece, HEAD_DIM), jnp.bfloat16),
        in_specs=[pl.BlockSpec(memory_space=pl.ANY)],
        out_specs=pl.BlockSpec(memory_space=pl.ANY),
        scratch_shapes=[
            pltpu.VMEM((3 * columns, own + 4, piece * height, HEAD_DIM), jnp.bfloat16),
            pltpu.VMEM((columns, own, piece * height, HEAD_DIM), jnp.bfloat16),
            pltpu.VMEM((3, 2 * unit, 18 * unit), jnp.float32),
            pltpu.VMEM((2 * unit, 128), jnp.float32),
            pltpu.VMEM((2, columns, own // 2 + 2, HEAD_DIM, 4 * unit), jnp.bfloat16),
            pltpu.VMEM((columns, own // 2 + 2, HEAD_DIM, 6 * unit), jnp.bfloat16),
            pltpu.SemaphoreType.DMA((len(PHASES), heads)),
            pltpu.SemaphoreType.DMA((len(PHASES), own * height)),
            pltpu.SemaphoreType.DMA((columns, own * height)),
            pltpu.SemaphoreType.DMA((columns, heads)),
            pltpu.SemaphoreType.DMA((2, 2)),
            pltpu.SemaphoreType.DMA((2, 2)),
        ],
        compiler_params=pltpu.CompilerParams(
            collective_id=0, has_side_effects=True, vmem_limit_bytes=56 * 1024 * 1024
        ),
    )(blocks)
    result = result.reshape(heads, columns, rows, frames, TILE_W, HEAD_DIM)
    return jnp.transpose(result, (3, 2, 1, 4, 0, 5)).reshape(frames, rows, cols, features)


def solution(mesh):
    band = P("tm", "height", None, None)
    return jax.shard_map(
        body,
        mesh=mesh,
        in_specs=(band, band, band),
        out_specs=band,
        check_vma=False,
    )
```

```python
import functools
import math
import types

import jax
import jax.numpy as jnp
from jax import lax
from jax.experimental import pallas as pl
from jax.experimental.pallas import tpu as pltpu
from jax.sharding import PartitionSpec as P

HEAD_DIM = 128
TILE_T = 6
TILE_H = 8
TILE_W = 8
BLOCK = 768
MESH = pl.DeviceIdType.MESH

KEY_BLOCK = (0, 1, 5)
VALUE_BLOCK = (2, 3, 6)
QUERY_BLOCK = (4, 7, 8)
ORDER = (("k", 0), ("k", 1), ("v", 0), ("v", 1), ("q", 0), ("k", 2), ("v", 2), ("q", 1), ("q", 2))
PHASES = ((0, 5), (5, 3), (8, 1))
HALO = ((0, 4), (5, 2))


def kernel(dims, x_ref, out_ref, y, o, even, odd, send, recv, osend, orecv, hsend, hrecv):
    heads, tm, height, frames, rows, tall = dims
    heads_here = heads // height
    group = tm // heads_here
    own = heads_here
    tiles = own * frames // TILE_T
    piece = frames * rows * TILE_W
    unit = frames * TILE_H * TILE_W
    scale = HEAD_DIM ** (-0.5) * math.log2(math.e)

    me_t, me_z = lax.axis_index("tm"), lax.axis_index("height")
    part = lax.rem(me_t, group)
    my_head = me_z * heads_here + me_t // group
    my_part = me_t // own
    my_slot = lax.rem(me_t, own)
    me = me_t * height + me_z
    hops = sorted(range(height), key=lambda hop: abs(hop - height / 2))

    stores = (even, odd)

    barrier = pltpu.get_barrier_semaphore()

    def greet(step, carry):
        other = lax.rem(me + step, tm * height)
        pl.semaphore_signal(
            barrier,
            inc=1,
            device_id={"tm": other // height, "height": lax.rem(other, height)},
            device_id_type=MESH,
        )
        return carry

    lax.fori_loop(1, tm * height, greet, 0)
    pl.semaphore_wait(barrier, tm * height - 1)

    def sending(phase, head):
        first, count = PHASES[phase]
        return pltpu.make_async_remote_copy(
            src_ref=x_ref.at[head, pl.ds(first, count)],
            dst_ref=y.at[pl.ds(first, count), 2 + my_slot, pl.ds(me_z * piece, piece), :],
            send_sem=send.at[phase, head],
            recv_sem=recv.at[phase, my_slot * height + me_z],
            device_id={"tm": lax.rem(head, heads_here) * group + my_part, "height": head // heads_here},
            device_id_type=MESH,
        )

    def keeping(phase):
        first, count = PHASES[phase]
        return pltpu.make_async_copy(
            x_ref.at[my_head, pl.ds(first, count)],
            y.at[pl.ds(first, count), 2 + my_slot, pl.ds(me_z * piece, piece), :],
            recv.at[phase, my_slot * height + me_z],
        )

    def is_me(head):
        return (head == my_head) & (part == my_part)

    def start_phase(phase):
        def one(step, carry):
            chip = lax.rem(me_t // group + step, heads_here)
            for hop in hops:
                head = lax.rem(me_z + hop, height) * heads_here + chip

                @pl.when(jnp.logical_not(is_me(head)))
                def _():
                    sending(phase, head).start()

                @pl.when(is_me(head))
                def _():
                    keeping(phase).start()

            return carry

        lax.fori_loop(0, heads_here, one, 0)

    def finish_sends(phase):
        def one(head, carry):
            @pl.when(jnp.logical_not(is_me(head)))
            def _():
                sending(phase, head).wait_send()

            return carry

        lax.fori_loop(0, heads, one, 0)

    def receive_phase(phase):
        first, count = PHASES[phase]

        def one(source, carry):
            slot, z = source // height, lax.rem(source, height)
            mine = (part * own + slot == me_t) & (z == me_z)

            @pl.when(mine)
            def _():
                keeping(phase).wait()

            @pl.when(jnp.logical_not(mine))
            def _():
                pltpu.make_async_remote_copy(
                    src_ref=x_ref.at[0, pl.ds(first, count)],
                    dst_ref=y.at[pl.ds(first, count), 2 + slot, pl.ds(z * piece, piece), :],
                    send_sem=send.at[phase, 0],
                    recv_sem=recv.at[phase, source],
                    device_id={"tm": part * own + slot, "height": z},
                    device_id_type=MESH,
                ).wait_recv()

            return carry

        lax.fori_loop(0, own * height, one, 0)

    def halo(phase, right):
        first, count = HALO[phase]
        source, target, to = (own, 0, me_t + 1) if right else (2, own + 2, me_t - 1)
        return pltpu.make_async_remote_copy(
            src_ref=y.at[pl.ds(first, count), pl.ds(source, 2)],
            dst_ref=y.at[pl.ds(first, count), pl.ds(target, 2)],
            send_sem=hsend.at[phase, int(right)],
            recv_sem=hrecv.at[phase, int(right)],
            device_id={"tm": to},
            device_id_type=MESH,
        )

    def exchange_halo(phase):
        @pl.when(part < group - 1)
        def _():
            halo(phase, True).start()

        @pl.when(part > 0)
        def _():
            halo(phase, False).start()

        @pl.when(part < group - 1)
        def _():
            halo(phase, False).wait_recv()

        @pl.when(part > 0)
        def _():
            halo(phase, True).wait_recv()

    def finish_halo(phase):
        @pl.when(part < group - 1)
        def _():
            halo(phase, True).wait_send()

        @pl.when(part > 0)
        def _():
            halo(phase, False).wait_send()

    def job_of(column, row, span, tile, scores):
        across = range(max(column - 1, 0), min(column + 2, 3))
        width = 2 * span * unit * len(across)
        blocks = [(low, min(low + BLOCK, width)) for low in range(0, width, BLOCK)]
        at = pl.ds(row * unit, unit)
        near = pl.ds(max(row - 1, 0) * unit, span * unit)
        query = jnp.concatenate(
            [y[QUERY_BLOCK[column], 2 + 2 * tile + half, at, :] for half in (0, 1)], axis=0
        )

        def gather(table, pair):
            return jnp.concatenate(
                [y[table[c], 2 * pair + half, near, :] for c in across for half in (0, 1)], axis=0
            )

        def score(pair, keys, index, largest):
            low, high = blocks[index]
            found = lax.dot_general(
                query, keys[low:high], (((1,), (1,)), ((), ())), preferred_element_type=jnp.float32
            )
            scores[pair - tile, :, low:high] = found
            for lane in range(0, high - low, 128):
                largest = jnp.maximum(largest, found[:, lane : lane + 128])
            return largest

        def weigh(pair, index, top):
            low, high = blocks[index]
            return jnp.exp2((scores[pair - tile, :, low:high] - top) * scale).astype(jnp.bfloat16)

        def add(weights, values, index, total):
            low, high = blocks[index]
            value = jnp.concatenate([values[low:high], jnp.ones((high - low, 128), jnp.bfloat16)], axis=1)
            return total + jnp.dot(weights, value, preferred_element_type=jnp.float32)

        def finish(total):
            result = (total[:, :128] / total[:, 128:]).astype(o.dtype)
            for half in (0, 1):
                o[column, 2 * tile + half, at, :] = result[half * unit : (half + 1) * unit]

        return types.SimpleNamespace(
            count=len(blocks), keys=lambda pair: gather(KEY_BLOCK, pair),
            values=lambda pair: gather(VALUE_BLOCK, pair), score=score, weigh=weigh, add=add, finish=finish,
        )

    def attend(column, tile):
        first_pair = tile + jnp.where((part == 0) & (tile == 0), 1, 0)
        last_pair = tile + jnp.where((part == group - 1) & (tile == tiles - 1), 2, 3)
        row_tiles = tall // TILE_H
        order = [(0, 2), (row_tiles - 1, 2)] + [(row, 3) for row in range(1, row_tiles - 1)]
        adding, top = None, None
        for index in range(len(order) + 1):
            scoring = None
            if index < len(order):
                scoring = job_of(column, *order[index], tile, stores[index % 2])

            def step(pair, carry, adding=adding, scoring=scoring, top=top):
                total, largest = carry
                if adding:
                    values = adding.values(pair)
                    weights = adding.weigh(pair, 0, top)
                if scoring:
                    keys = scoring.keys(pair)
                for block in range(max(job.count for job in (adding, scoring) if job)):
                    if scoring and block < scoring.count:
                        largest = scoring.score(pair, keys, block, largest)
                    if adding and block < adding.count:
                        current = weights
                        if block + 1 < adding.count:
                            weights = adding.weigh(pair, block + 1, top)
                        total = adding.add(current, values, block, total)
                return total, largest

            total = jnp.zeros((2 * unit, 256), jnp.float32) if adding else None
            largest = jnp.full((2 * unit, 128), -jnp.inf, jnp.float32) if scoring else None
            total, largest = lax.fori_loop(first_pair, last_pair, step, (total, largest))
            if adding:
                adding.finish(total)
            if scoring:
                top = jnp.max(largest, axis=1, keepdims=True)
            adding = scoring

    def attend_column(column):
        def one(step, carry):
            tile = jnp.where(lax.rem(part, 2) == 0, step, tiles - 1 - step)
            attend(column, tile)
            return_tile(column, tile)
            return carry

        lax.fori_loop(0, tiles, one, 0)

    def returning(column, source):
        slot, z = source // height, lax.rem(source, height)
        return pltpu.make_async_remote_copy(
            src_ref=o.at[column, slot, pl.ds(z * piece, piece), :],
            dst_ref=out_ref.at[my_head, column],
            send_sem=osend.at[column, source],
            recv_sem=orecv.at[column, my_head],
            device_id={"tm": part * own + slot, "height": z},
            device_id_type=MESH,
        )

    def returning_here(column):
        return pltpu.make_async_copy(
            o.at[column, my_slot, pl.ds(me_z * piece, piece), :],
            out_ref.at[my_head, column],
            orecv.at[column, my_head],
        )

    def source_is_me(source):
        return (part * own + source // height == me_t) & (lax.rem(source, height) == me_z)

    def return_tile(column, tile):
        def one(step, carry):
            z = lax.rem(me_z + height // 2 + step // 2, height)
            source = (2 * tile + lax.rem(step, 2)) * height + z

            @pl.when(jnp.logical_not(source_is_me(source)))
            def _():
                returning(column, source).start()

            @pl.when(source_is_me(source))
            def _():
                returning_here(column).start()

            return carry

        lax.fori_loop(0, 2 * height, one, 0)

    def finish_column(column):
        def sent(source, carry):
            @pl.when(jnp.logical_not(source_is_me(source)))
            def _():
                returning(column, source).wait_send()

            return carry

        lax.fori_loop(0, own * height, sent, 0)

        def landed(head, carry):
            @pl.when(is_me(head))
            def _():
                returning_here(column).wait()

            @pl.when(jnp.logical_not(is_me(head)))
            def _():
                pltpu.make_async_remote_copy(
                    src_ref=o.at[column, 0, pl.ds(0, piece), :],
                    dst_ref=out_ref.at[head, column],
                    send_sem=osend.at[column, 0],
                    recv_sem=orecv.at[column, head],
                    device_id={"tm": lax.rem(head, heads_here) * group + my_part, "height": head // heads_here},
                    device_id_type=MESH,
                ).wait_recv()

            return carry

        lax.fori_loop(0, heads, landed, 0)

    for phase in range(len(PHASES)):
        start_phase(phase)
    for phase in range(len(PHASES)):
        receive_phase(phase)
        if phase < len(HALO):
            exchange_halo(phase)
        attend_column(phase)
    for phase in range(len(PHASES)):
        finish_sends(phase)
    for phase in range(len(HALO)):
        finish_halo(phase)
    for column in (0, 1, 2):
        finish_column(column)


def body(query_band, key_band, value_band):
    frames, rows, cols, features = query_band.shape
    heads = features // HEAD_DIM
    tm, height = lax.axis_size("tm"), lax.axis_size("height")
    columns = cols // TILE_W
    piece = frames * rows * TILE_W
    tall = rows * height
    own = heads // height

    def by_head(value):
        value = value.reshape(frames, rows, columns, TILE_W, heads, HEAD_DIM)
        return jnp.transpose(value, (4, 2, 1, 0, 3, 5)).reshape(heads, columns, piece, HEAD_DIM)

    bands = {"q": by_head(query_band), "k": by_head(key_band), "v": by_head(value_band)}
    blocks = jnp.stack([bands[name][:, column] for name, column in ORDER], axis=1)

    unit = frames * TILE_H * TILE_W
    dims = (heads, tm, height, frames, rows, tall)
    result = pl.pallas_call(
        functools.partial(kernel, dims),
        out_shape=jax.ShapeDtypeStruct((heads, columns, piece, HEAD_DIM), jnp.bfloat16),
        in_specs=[pl.BlockSpec(memory_space=pl.ANY)],
        out_specs=pl.BlockSpec(memory_space=pl.ANY),
        scratch_shapes=[
            pltpu.VMEM((3 * columns, own + 4, piece * height, HEAD_DIM), jnp.bfloat16),
            pltpu.VMEM((columns, own, piece * height, HEAD_DIM), jnp.bfloat16),
            pltpu.VMEM((3, 2 * unit, 18 * unit), jnp.float32),
            pltpu.VMEM((3, 2 * unit, (12 if tall == 3 * TILE_H else 18) * unit), jnp.float32),
            pltpu.SemaphoreType.DMA((len(PHASES), heads)),
            pltpu.SemaphoreType.DMA((len(PHASES), own * height)),
            pltpu.SemaphoreType.DMA((columns, own * height)),
            pltpu.SemaphoreType.DMA((columns, heads)),
            pltpu.SemaphoreType.DMA((2, 2)),
            pltpu.SemaphoreType.DMA((2, 2)),
        ],
        compiler_params=pltpu.CompilerParams(
            collective_id=0, has_side_effects=True, vmem_limit_bytes=56 * 1024 * 1024
        ),
    )(blocks)
    result = result.reshape(heads, columns, rows, frames, TILE_W, HEAD_DIM)
    return jnp.transpose(result, (3, 2, 1, 4, 0, 5)).reshape(frames, rows, cols, features)


def solution(mesh):
    band = P("tm", "height", None, None)
    return jax.shard_map(
        body,
        mesh=mesh,
        in_specs=(band, band, band),
        out_specs=band,
        check_vma=False,
    )
```

```python
import functools
import math
import types

import jax
import jax.numpy as jnp
from jax import lax
from jax.experimental import pallas as pl
from jax.experimental.pallas import tpu as pltpu
from jax.sharding import PartitionSpec as P

HEAD_DIM = 128
TILE_T = 6
TILE_H = 8
TILE_W = 8
BLOCK = 768
MESH = pl.DeviceIdType.MESH

KEY_BLOCK = (0, 1, 5)
VALUE_BLOCK = (2, 3, 6)
QUERY_BLOCK = (4, 7, 8)
ORDER = (("k", 0), ("k", 1), ("v", 0), ("v", 1), ("q", 0), ("k", 2), ("v", 2), ("q", 1), ("q", 2))
PHASES = ((0, 5), (5, 3), (8, 1))
HALO = ((0, 4), (5, 2))


def kernel(dims, x_ref, out_ref, y, o, even, odd, send, recv, osend, orecv, hsend, hrecv):
    heads, tm, height, frames, rows, tall = dims
    heads_here = heads // height
    group = tm // heads_here
    own = heads_here
    tiles = own * frames // TILE_T
    piece = frames * rows * TILE_W
    unit = frames * TILE_H * TILE_W
    scale = HEAD_DIM ** (-0.5) * math.log2(math.e)

    me_t, me_z = lax.axis_index("tm"), lax.axis_index("height")
    part = lax.rem(me_t, group)
    my_head = me_z * heads_here + me_t // group
    my_part = me_t // own
    my_slot = lax.rem(me_t, own)
    me = me_t * height + me_z
    hops = sorted(range(height), key=lambda hop: abs(hop - height / 2))

    stores = (even, odd)

    barrier = pltpu.get_barrier_semaphore()

    def greet(step, carry):
        other = lax.rem(me + step, tm * height)
        pl.semaphore_signal(
            barrier,
            inc=1,
            device_id={"tm": other // height, "height": lax.rem(other, height)},
            device_id_type=MESH,
        )
        return carry

    lax.fori_loop(1, tm * height, greet, 0)
    pl.semaphore_wait(barrier, tm * height - 1)

    def sending(phase, head):
        first, count = PHASES[phase]
        return pltpu.make_async_remote_copy(
            src_ref=x_ref.at[head, pl.ds(first, count)],
            dst_ref=y.at[pl.ds(first, count), 2 + my_slot, pl.ds(me_z * piece, piece), :],
            send_sem=send.at[phase, head],
            recv_sem=recv.at[phase, my_slot * height + me_z],
            device_id={"tm": lax.rem(head, heads_here) * group + my_part, "height": head // heads_here},
            device_id_type=MESH,
        )

    def keeping(phase):
        first, count = PHASES[phase]
        return pltpu.make_async_copy(
            x_ref.at[my_head, pl.ds(first, count)],
            y.at[pl.ds(first, count), 2 + my_slot, pl.ds(me_z * piece, piece), :],
            recv.at[phase, my_slot * height + me_z],
        )

    def is_me(head):
        return (head == my_head) & (part == my_part)

    def start_phase(phase):
        def one(step, carry):
            chip = lax.rem(me_t // group + step, heads_here)
            for hop in hops:
                head = lax.rem(me_z + hop, height) * heads_here + chip

                @pl.when(jnp.logical_not(is_me(head)))
                def _():
                    sending(phase, head).start()

                @pl.when(is_me(head))
                def _():
                    keeping(phase).start()

            return carry

        lax.fori_loop(0, heads_here, one, 0)

    def finish_sends(phase):
        def one(head, carry):
            @pl.when(jnp.logical_not(is_me(head)))
            def _():
                sending(phase, head).wait_send()

            return carry

        lax.fori_loop(0, heads, one, 0)

    def receive_phase(phase):
        first, count = PHASES[phase]

        def one(source, carry):
            slot, z = source // height, lax.rem(source, height)
            mine = (part * own + slot == me_t) & (z == me_z)

            @pl.when(mine)
            def _():
                keeping(phase).wait()

            @pl.when(jnp.logical_not(mine))
            def _():
                pltpu.make_async_remote_copy(
                    src_ref=x_ref.at[0, pl.ds(first, count)],
                    dst_ref=y.at[pl.ds(first, count), 2 + slot, pl.ds(z * piece, piece), :],
                    send_sem=send.at[phase, 0],
                    recv_sem=recv.at[phase, source],
                    device_id={"tm": part * own + slot, "height": z},
                    device_id_type=MESH,
                ).wait_recv()

            return carry

        lax.fori_loop(0, own * height, one, 0)

    def halo(phase, right):
        first, count = HALO[phase]
        source, target, to = (own, 0, me_t + 1) if right else (2, own + 2, me_t - 1)
        return pltpu.make_async_remote_copy(
            src_ref=y.at[pl.ds(first, count), pl.ds(source, 2)],
            dst_ref=y.at[pl.ds(first, count), pl.ds(target, 2)],
            send_sem=hsend.at[phase, int(right)],
            recv_sem=hrecv.at[phase, int(right)],
            device_id={"tm": to},
            device_id_type=MESH,
        )

    def exchange_halo(phase):
        @pl.when(part < group - 1)
        def _():
            halo(phase, True).start()

        @pl.when(part > 0)
        def _():
            halo(phase, False).start()

        @pl.when(part < group - 1)
        def _():
            halo(phase, False).wait_recv()

        @pl.when(part > 0)
        def _():
            halo(phase, True).wait_recv()

    def finish_halo(phase):
        @pl.when(part < group - 1)
        def _():
            halo(phase, True).wait_send()

        @pl.when(part > 0)
        def _():
            halo(phase, False).wait_send()

    def job_of(column, row, span, tile, scores):
        across = range(max(column - 1, 0), min(column + 2, 3))
        width = 2 * span * unit * len(across)
        blocks = [(low, min(low + BLOCK, width)) for low in range(0, width, BLOCK)]
        at = pl.ds(row * unit, unit)
        near = pl.ds(max(row - 1, 0) * unit, span * unit)
        query = jnp.concatenate(
            [y[QUERY_BLOCK[column], 2 + 2 * tile + half, at, :] for half in (0, 1)], axis=0
        )

        def gather(table, pair):
            return jnp.concatenate(
                [y[table[c], 2 * pair + half, near, :] for c in across for half in (0, 1)], axis=0
            )

        def score(pair, keys, index, largest):
            low, high = blocks[index]
            found = lax.dot_general(
                query, keys[low:high], (((1,), (1,)), ((), ())), preferred_element_type=jnp.float32
            )
            scores[pair - tile, :, low:high] = found
            for lane in range(0, high - low, 128):
                largest = jnp.maximum(largest, found[:, lane : lane + 128])
            return largest

        def weigh(pair, index, top):
            low, high = blocks[index]
            return jnp.exp2((scores[pair - tile, :, low:high] - top) * scale).astype(jnp.bfloat16)

        def add(weights, values, index, total):
            low, high = blocks[index]
            value = jnp.concatenate([values[low:high], jnp.ones((high - low, 128), jnp.bfloat16)], axis=1)
            return total + jnp.dot(weights, value, preferred_element_type=jnp.float32)

        def finish(total):
            result = (total[:, :128] / total[:, 128:]).astype(o.dtype)
            for half in (0, 1):
                o[column, 2 * tile + half, at, :] = result[half * unit : (half + 1) * unit]

        return types.SimpleNamespace(
            count=len(blocks), keys=lambda pair: gather(KEY_BLOCK, pair),
            values=lambda pair: gather(VALUE_BLOCK, pair), score=score, weigh=weigh, add=add, finish=finish,
        )

    def attend(column, tile):
        first_pair = tile + jnp.where((part == 0) & (tile == 0), 1, 0)
        last_pair = tile + jnp.where((part == group - 1) & (tile == tiles - 1), 2, 3)
        row_tiles = tall // TILE_H
        order = [(0, 2), (row_tiles - 1, 2)] + [(row, 3) for row in range(1, row_tiles - 1)]
        adding, top = None, None
        for index in range(len(order) + 1):
            scoring = None
            if index < len(order):
                scoring = job_of(column, *order[index], tile, stores[index % 2])

            def step(pair, carry, adding=adding, scoring=scoring, top=top):
                total, largest = carry
                if adding:
                    values = adding.values(pair)
                    weights = adding.weigh(pair, 0, top)
                if scoring:
                    keys = scoring.keys(pair)
                for block in range(max(job.count for job in (adding, scoring) if job)):
                    if scoring and block < scoring.count:
                        largest = scoring.score(pair, keys, block, largest)
                    if adding and block < adding.count:
                        current = weights
                        if block + 1 < adding.count:
                            weights = adding.weigh(pair, block + 1, top)
                        total = adding.add(current, values, block, total)
                return total, largest

            total = jnp.zeros((2 * unit, 256), jnp.float32) if adding else None
            largest = jnp.full((2 * unit, 128), -jnp.inf, jnp.float32) if scoring else None
            total, largest = lax.fori_loop(first_pair, last_pair, step, (total, largest))
            if adding:
                adding.finish(total)
            if scoring:
                top = jnp.max(largest, axis=1, keepdims=True)
            adding = scoring

    def attend_column(column):
        def one(step, carry):
            tile = jnp.where(lax.rem(part, 2) == 0, step, tiles - 1 - step)
            attend(column, tile)
            if column > 0:
                return_tile(column, tile)
            return carry

        lax.fori_loop(0, tiles, one, 0)

    def returning(column, source):
        slot, z = source // height, lax.rem(source, height)
        return pltpu.make_async_remote_copy(
            src_ref=o.at[column, slot, pl.ds(z * piece, piece), :],
            dst_ref=out_ref.at[my_head, column],
            send_sem=osend.at[column, source],
            recv_sem=orecv.at[column, my_head],
            device_id={"tm": part * own + slot, "height": z},
            device_id_type=MESH,
        )

    def returning_here(column):
        return pltpu.make_async_copy(
            o.at[column, my_slot, pl.ds(me_z * piece, piece), :],
            out_ref.at[my_head, column],
            orecv.at[column, my_head],
        )

    def source_is_me(source):
        return (part * own + source // height == me_t) & (lax.rem(source, height) == me_z)

    def return_tile(column, tile):
        def one(step, carry):
            z = lax.rem(me_z + height // 2 + step // 2, height)
            source = (2 * tile + lax.rem(step, 2)) * height + z

            @pl.when(jnp.logical_not(source_is_me(source)))
            def _():
                returning(column, source).start()

            @pl.when(source_is_me(source))
            def _():
                returning_here(column).start()

            return carry

        lax.fori_loop(0, 2 * height, one, 0)

    def finish_column(column):
        def sent(source, carry):
            @pl.when(jnp.logical_not(source_is_me(source)))
            def _():
                returning(column, source).wait_send()

            return carry

        lax.fori_loop(0, own * height, sent, 0)

        def landed(head, carry):
            @pl.when(is_me(head))
            def _():
                returning_here(column).wait()

            @pl.when(jnp.logical_not(is_me(head)))
            def _():
                pltpu.make_async_remote_copy(
                    src_ref=o.at[column, 0, pl.ds(0, piece), :],
                    dst_ref=out_ref.at[head, column],
                    send_sem=osend.at[column, 0],
                    recv_sem=orecv.at[column, head],
                    device_id={"tm": lax.rem(head, heads_here) * group + my_part, "height": head // heads_here},
                    device_id_type=MESH,
                ).wait_recv()

            return carry

        lax.fori_loop(0, heads, landed, 0)

    start_phase(0)
    finish_sends(0)
    start_phase(1)
    receive_phase(0)
    exchange_halo(0)
    attend_column(0)
    receive_phase(1)
    start_phase(2)
    for tile in range(tiles):
        return_tile(0, tile)
    exchange_halo(1)
    attend_column(1)
    receive_phase(2)
    attend_column(2)
    finish_sends(1)
    finish_sends(2)
    for phase in range(len(HALO)):
        finish_halo(phase)
    for column in (0, 1, 2):
        finish_column(column)


def body(query_band, key_band, value_band):
    frames, rows, cols, features = query_band.shape
    heads = features // HEAD_DIM
    tm, height = lax.axis_size("tm"), lax.axis_size("height")
    columns = cols // TILE_W
    piece = frames * rows * TILE_W
    tall = rows * height
    own = heads // height

    def by_head(value):
        value = value.reshape(frames, rows, columns, TILE_W, heads, HEAD_DIM)
        return jnp.transpose(value, (4, 2, 1, 0, 3, 5)).reshape(heads, columns, piece, HEAD_DIM)

    bands = {"q": by_head(query_band), "k": by_head(key_band), "v": by_head(value_band)}
    blocks = jnp.stack([bands[name][:, column] for name, column in ORDER], axis=1)

    unit = frames * TILE_H * TILE_W
    dims = (heads, tm, height, frames, rows, tall)
    result = pl.pallas_call(
        functools.partial(kernel, dims),
        out_shape=jax.ShapeDtypeStruct((heads, columns, piece, HEAD_DIM), jnp.bfloat16),
        in_specs=[pl.BlockSpec(memory_space=pl.ANY)],
        out_specs=pl.BlockSpec(memory_space=pl.ANY),
        scratch_shapes=[
            pltpu.VMEM((3 * columns, own + 4, piece * height, HEAD_DIM), jnp.bfloat16),
            pltpu.VMEM((columns, own, piece * height, HEAD_DIM), jnp.bfloat16),
            pltpu.VMEM((3, 2 * unit, 18 * unit), jnp.float32),
            pltpu.VMEM((3, 2 * unit, (12 if tall == 3 * TILE_H else 18) * unit), jnp.float32),
            pltpu.SemaphoreType.DMA((len(PHASES), heads)),
            pltpu.SemaphoreType.DMA((len(PHASES), own * height)),
            pltpu.SemaphoreType.DMA((columns, own * height)),
            pltpu.SemaphoreType.DMA((columns, heads)),
            pltpu.SemaphoreType.DMA((2, 2)),
            pltpu.SemaphoreType.DMA((2, 2)),
        ],
        compiler_params=pltpu.CompilerParams(
            collective_id=0, has_side_effects=True, vmem_limit_bytes=48 * 1024 * 1024
        ),
    )(blocks)
    result = result.reshape(heads, columns, rows, frames, TILE_W, HEAD_DIM)
    return jnp.transpose(result, (3, 2, 1, 4, 0, 5)).reshape(frames, rows, cols, features)


def solution(mesh):
    band = P("tm", "height", None, None)
    return jax.shard_map(
        body,
        mesh=mesh,
        in_specs=(band, band, band),
        out_specs=band,
        check_vma=False,
    )
```
